128 devices in a mesh: basis: 32 (over x, z, core), aux: 4 (over y).
Axes of the slice: x: 4, y: 4, z: 4, core: 2. Of those that a mesh axis runs over, the one named last changes fastest.
Arguments:
- factors: bfloat16 [65536, 16, 200], P('basis', 'aux'), may hold values from -0.09375 to 0.09375
- orbitals: bfloat16 [65536, 200], P('basis'), may hold values from -6 to 6
- block_slot: int32 [256], replicated, may hold values from 0 to 255, as said below
- pair_list: int32 [2048, 2], replicated, may hold values from 0 to 255, as said below
- pair_owner: int32 [2048], replicated, may hold values from -1 to 31, as said below
Outputs:
- exchange_product: bfloat16 [65536, 200], P('basis')
The draws below stay inside these ranges and needn't reach their ends.
Inputs may be any that keep to these rules, and one draw needn't show every extreme that they name: `block_slot`: a permutation of the 256 shell blocks onto the 256 storage slots. `pair_list`: each entry names two different shell blocks, the smaller first. Over the live pairs of one owner, the blocks stored on any one index of basis number at most 2, and some owner reaches 2 from some index. `pair_owner`: each index of basis owns at most 64 live pairs, and one owns exactly 64.
All inputs are finite; a program needn't handle non-finite values.
Results may differ from the reference program's by a relative error of at most 0.0057.
Values may be sent and summed in bfloat16 or wider, within the bound.
No kernel may reach another device: no remote copies, remote signals or barrier semaphores. Data moves between devices by JAX's collectives and lax.ppermute only.
A program may use at most 256 MiB of HBM per device.

```python
import jax
import jax.numpy as jnp
from jax import lax

BLOCK = 256
OCC = 200
AUX = 16
BLK_DEV = 8
PAIR_CAP = 64
NBLK = 256
NROWS = 65536
N_BASIS = 32
N_AUX = 4


def pair_tables(key):
    keys = jax.random.split(key, 9)
    slot_of_block = jax.random.permutation(keys[0], NBLK).astype(jnp.int32)
    block_at_slot = jnp.zeros((NBLK,), jnp.int32).at[slot_of_block].set(jnp.arange(NBLK, dtype=jnp.int32))
    shape = (N_BASIS, N_BASIS)
    first = jax.random.randint(keys[1], shape, 0, BLK_DEV)
    offset = jax.random.randint(keys[2], shape, 1, BLK_DEV)
    second = (first + offset) % BLK_DEV
    extra = jax.random.randint(keys[3], shape, 0, 2)
    forced = jax.random.randint(keys[4], (N_BASIS,), 0, N_BASIS)
    sources = jnp.broadcast_to(jnp.arange(N_BASIS, dtype=jnp.int32)[None, :], shape)
    extra = jnp.where(sources == forced[:, None], 1, extra)
    pool = jnp.stack([sources * BLK_DEV + first, sources * BLK_DEV + second], axis=2).reshape(N_BASIS, 2 * N_BASIS)
    alive = jnp.stack([jnp.ones_like(extra), extra], axis=2).reshape(N_BASIS, 2 * N_BASIS)
    shuffles = jax.vmap(lambda k: jax.random.permutation(k, 2 * N_BASIS))(jax.random.split(keys[5], N_BASIS))
    order = jnp.argsort((1 - alive) * (2 * N_BASIS) + shuffles, axis=1, stable=True)
    pool = jnp.take_along_axis(pool, order, axis=1)
    count_live = jnp.sum(alive, axis=1)[:, None]
    counts = jax.random.randint(keys[6], (N_BASIS,), PAIR_CAP // 4, PAIR_CAP + 1)
    full = jax.random.randint(keys[7], (), 0, N_BASIS)
    owners = jnp.arange(N_BASIS, dtype=jnp.int32)
    counts = jnp.where(owners == full, PAIR_CAP, counts)
    turn = jnp.arange(PAIR_CAP, dtype=jnp.int32)[None, :]
    entry_one = turn % count_live
    entry_two = (turn + 1 + turn // count_live % (count_live - 1)) % count_live
    block_one = block_at_slot[jnp.take_along_axis(pool, entry_one, axis=1)]
    block_two = block_at_slot[jnp.take_along_axis(pool, entry_two, axis=1)]
    low = jnp.minimum(block_one, block_two)
    high = jnp.maximum(block_one, block_two)
    owner = jnp.where(turn < counts[:, None], owners[:, None], -1)
    mix = jax.random.permutation(keys[8], N_BASIS * PAIR_CAP)
    pairs = jnp.stack([low, high], axis=2).reshape(N_BASIS * PAIR_CAP, 2)[mix]
    owner = owner.reshape(N_BASIS * PAIR_CAP)[mix]
    return (slot_of_block.astype(jnp.int32), pairs.astype(jnp.int32), owner.astype(jnp.int32))


def draw_block_slot(key, part):
    tables = pair_tables(key)
    return tables[0]


def draw_pair_list(key, part):
    tables = pair_tables(key)
    return tables[1]


def draw_pair_owner(key, part):
    tables = pair_tables(key)
    return tables[2]


def levels(rng, shape, cuts, low, top_value):
    def one(position, blocks):
        heights = jax.random.uniform(jax.random.fold_in(jax.random.fold_in(rng, 6), position), (blocks,), jnp.float32, low / len(cuts), top_value / len(cuts))
        return jnp.repeat(jnp.exp(heights), shape[position] // blocks).reshape((-1,) + (1,) * (len(shape) - position - 1))

    loudness = one(*cuts[0])
    for cut in cuts[1:]:
        loudness = loudness * one(*cut)
    return loudness


def centred(rng, shape, spread, bound, cuts=(), held_as=jnp.bfloat16):
    values = jax.random.normal(rng, shape, jnp.float32) * spread
    if len(cuts) > 0:
        values = levels(rng, shape, cuts, -0.22, 0.18) * values
    return jnp.clip(values, min=-bound, max=bound).astype(held_as)


def setup_inputs(seed: int = 0) -> dict:
    seeds = jax.random.split(jax.random.key(seed), 6)
    factors = centred(seeds[0], (NROWS, AUX, OCC), 0.015, 0.09375, ((0, 32), (1, 4)))
    orbitals = centred(seeds[1], (NROWS, OCC), 1.0, 6.0, ((0, 32),))
    block_slot = draw_block_slot(jax.random.fold_in(seeds[5], 71), 0)
    pair_list = draw_pair_list(jax.random.fold_in(seeds[5], 71), 0)
    pair_owner = draw_pair_owner(jax.random.fold_in(seeds[5], 71), 0)
    return {"factors": factors, "orbitals": orbitals, "block_slot": block_slot, "pair_list": pair_list, "pair_owner": pair_owner}


def reference(factors, orbitals, block_slot, pair_list, pair_owner):
    per = AUX // N_AUX
    blocks = factors.reshape(NBLK, BLOCK, N_AUX, per * OCC)
    rows_x = orbitals.reshape(NBLK, BLOCK, OCC)
    slot_a = block_slot[pair_list[:, 0]]
    slot_b = block_slot[pair_list[:, 1]]
    group = 8

    def owner_term(total, owner):
        mine = pair_owner == owner
        picked = jnp.nonzero(mine, size=PAIR_CAP, fill_value=0)[0].astype(jnp.int32)
        weight = mine[picked].astype(jnp.float32)
        first = slot_a[picked]
        second = slot_b[picked]
        for part in range(N_AUX):
            def pair_step(acc, turn):
                start = turn * group
                ra = lax.dynamic_slice_in_dim(first, start, group)
                rb = lax.dynamic_slice_in_dim(second, start, group)
                wt = lax.dynamic_slice_in_dim(weight, start, group)
                left = blocks[ra, :, part].astype(jnp.float32)
                right = blocks[rb, :, part].astype(jnp.float32)
                tile = jnp.einsum('gmk,gnk->gmn', left, right).astype(jnp.bfloat16).astype(jnp.float32)
                xa = rows_x[ra].astype(jnp.float32)
                xb = rows_x[rb].astype(jnp.float32)
                to_a = jnp.einsum('gmn,gnj->gmj', tile, xb) * wt[:, None, None]
                to_b = jnp.einsum('gmn,gmj->gnj', tile, xa) * wt[:, None, None]
                return acc.at[ra].add(to_a).at[rb].add(to_b), None

            acc, _ = lax.scan(pair_step, jnp.zeros((NBLK, BLOCK, OCC), jnp.float32),
                              jnp.arange(PAIR_CAP // group, dtype=jnp.int32))
            total = total + lax.optimization_barrier(acc.astype(jnp.bfloat16)).astype(jnp.float32)
        return total, None

    total, _ = lax.scan(owner_term, jnp.zeros((NBLK, BLOCK, OCC), jnp.float32),
                        jnp.arange(N_BASIS, dtype=jnp.int32))
    return total.astype(jnp.bfloat16).reshape(NBLK * BLOCK, OCC)
```

```python
import functools

import jax
import jax.numpy as jnp
from jax import lax
from jax.experimental import pallas as pl
from jax.experimental.pallas import tpu as pltpu
from jax.sharding import PartitionSpec as P

BLOCK = 256
PAIR_CAP = 64
LANES = 128
CHUNKS = ((0, 200),)
VMEM = 56 * 1024 * 1024


def plan(span, depth, ndev):
    full = depth // LANES
    rest = depth - full * LANES
    fold = LANES // rest
    group = -(-span // (fold * 8)) * 8
    rows = full * span + group
    per = -(-rows // ndev)
    return full, rest, fold, group, per


def count_kernel(slot_ref, pairs_ref, owner_ref, low_ref, high_ref, flag_ref):
    nblk = slot_ref.shape[1]
    npair = pairs_ref.shape[1]
    ids = lax.broadcasted_iota(jnp.int32, (nblk, npair), 0)
    owner = owner_ref[...]
    held = jnp.sum((owner == owner_ref[0:1, 0:1]).astype(jnp.float32), axis=1, keepdims=True)
    entry = lax.broadcasted_iota(jnp.int32, (1, npair), 1)
    weight = jnp.where(entry == 0, PAIR_CAP + 1.0 - held, 1.0)
    weight = jnp.where(owner >= 0, weight, 0.0)
    one_a = jnp.where(ids == pairs_ref[0:1, :], weight, 0.0).astype(jnp.bfloat16)
    one_b = (ids == pairs_ref[1:2, :]).astype(jnp.float32).astype(jnp.bfloat16)
    rows = lax.broadcasted_iota(jnp.int32, (nblk, nblk), 0)
    place = (rows == slot_ref[...]).astype(jnp.float32).astype(jnp.bfloat16)
    at = jnp.dot(place, one_a, preferred_element_type=jnp.float32).astype(jnp.bfloat16)
    bt = jnp.dot(place, one_b, preferred_element_type=jnp.float32).astype(jnp.bfloat16)
    dims = (((1,), (1,)), ((), ()))
    count = lax.dot_general(at, bt, dims, preferred_element_type=jnp.float32)
    count += lax.dot_general(bt, at, dims, preferred_element_type=jnp.float32)
    high = jnp.floor(count * (1.0 / 256.0)) * 256.0
    low_ref[...] = (count - high).astype(jnp.bfloat16)
    high_ref[...] = high.astype(jnp.bfloat16)
    flag_ref[0] = (jnp.max(high) > 0).astype(jnp.int32)


def pair_counts(block_slot, pair_list, pair_owner):
    nblk = block_slot.shape[0]
    square = jax.ShapeDtypeStruct((nblk, nblk), jnp.bfloat16)
    vmem = pl.BlockSpec(memory_space=pltpu.VMEM)
    return pl.pallas_call(
        count_kernel,
        out_shape=(square, square, jax.ShapeDtypeStruct((1,), jnp.int32)),
        in_specs=[vmem] * 3,
        out_specs=(vmem, vmem, pl.BlockSpec(memory_space=pltpu.SMEM)),
        compiler_params=pltpu.CompilerParams(vmem_limit_bytes=VMEM),
        name="pair_counts",
    )(block_slot[None, :], pair_list.T, pair_owner[None, :])


def pack_kernel(spans, plans, ndev, x_ref, f_ref, *refs):
    outs, scratch = refs[: len(spans)], refs[len(spans):]
    b = pl.program_id(0)
    dims = (((1,), (1,)), ((), ()))
    for (lo, hi), (full, rest, fold, group, per), stage in zip(spans, plans, scratch):
        span = hi - lo
        x = x_ref[lo:hi, :]
        for t in range(0, full, 2):
            g = lax.dot_general(
                x, f_ref[t * LANES : (t + 2) * LANES, :], dims, preferred_element_type=jnp.float32
            )
            for half in range(2):
                stage[pl.ds((t + half) * span * 8 + b, span, stride=8), :] = g[
                    :, half * LANES : (half + 1) * LANES
                ]
        g = lax.dot_general(
            x, f_ref[full * LANES :, :], dims, preferred_element_type=jnp.float32
        )
        short = fold * group - span
        if short:
            g = jnp.concatenate([g, jnp.zeros((short, rest), jnp.float32)], axis=0)
        g = jnp.concatenate([g[q * group : (q + 1) * group] for q in range(fold)], axis=1)
        stage[pl.ds(full * span * 8 + b, group, stride=8), :] = g

    @pl.when(b == pl.num_programs(0) - 1)
    def _():
        for (lo, hi), (full, rest, fold, group, per), stage, out in zip(spans, plans, scratch, outs):
            rows = full * (hi - lo) + group
            out[0:rows] = stage[...].reshape(rows, 8, LANES).astype(jnp.bfloat16)


def pack(xt, ft, spans, plans, ndev):
    depth, width = ft.shape
    blocks = width // BLOCK
    outs = [jax.ShapeDtypeStruct((ndev * p[4], blocks, LANES), jnp.bfloat16) for p in plans]
    return pl.pallas_call(
        functools.partial(pack_kernel, spans, plans, ndev),
        out_shape=outs,
        grid=(blocks,),
        in_specs=[
            pl.BlockSpec((xt.shape[0], BLOCK), lambda b: (0, b)),
            pl.BlockSpec((depth, BLOCK), lambda b: (0, b)),
        ],
        out_specs=[pl.BlockSpec(o.shape, lambda b: (0, 0, 0)) for o in outs],
        scratch_shapes=[
            pltpu.VMEM(((p[0] * (s[1] - s[0]) + p[3]) * 8, LANES), jnp.float32)
            for s, p in zip(spans, plans)
        ],
        compiler_params=pltpu.CompilerParams(vmem_limit_bytes=VMEM),
        name="pack",
    )(xt, ft)


def mix_kernel(flag_ref, low_ref, high_ref, g_ref, h_ref):
    ndev, per, blocks, lanes = g_ref.shape
    nblk = ndev * blocks

    def tile(t, use_high):
        g = g_ref[:, t].astype(jnp.float32).reshape(nblk, lanes).astype(jnp.bfloat16)
        h = jnp.dot(low_ref[...], g, preferred_element_type=jnp.float32)
        if use_high:
            h += jnp.dot(high_ref[...], g, preferred_element_type=jnp.float32)
        h_ref[:, t] = h.reshape(ndev, blocks, lanes).astype(jnp.bfloat16)

    @pl.when(flag_ref[0] == 0)
    def _():
        for t in range(per):
            tile(t, False)

    @pl.when(flag_ref[0] != 0)
    def _():
        for t in range(per):
            tile(t, True)


def mix(counts, g):
    low, high, flag = counts
    vmem = pl.BlockSpec(memory_space=pltpu.VMEM)
    return pl.pallas_call(
        mix_kernel,
        out_shape=jax.ShapeDtypeStruct(g.shape, jnp.bfloat16),
        in_specs=[pl.BlockSpec(memory_space=pltpu.SMEM), vmem, vmem, vmem],
        out_specs=vmem,
        compiler_params=pltpu.CompilerParams(vmem_limit_bytes=VMEM),
        name="mix",
    )(flag, low, high, g)


def apply_kernel(span, parts, h_ref, f_ref, e_ref, stage):
    full, rest, fold, group, per = parts
    a = pl.program_id(0)
    rows = full * span + group

    @pl.when(a == 0)
    def _():
        stage[...] = h_ref[0:rows].astype(jnp.float32).reshape(rows * 8, LANES)

    total = jnp.zeros((span, BLOCK), jnp.float32)
    for t in range(0, full, 2):
        left = jnp.concatenate(
            [
                stage[pl.ds((t + half) * span * 8 + a, span, stride=8), :].astype(jnp.bfloat16)
                for half in range(2)
            ],
            axis=1,
        )
        total += jnp.dot(
            left, f_ref[t * LANES : (t + 2) * LANES, :], preferred_element_type=jnp.float32
        )
    left = stage[pl.ds(full * span * 8 + a, group, stride=8), :]
    left = jnp.concatenate([left[:, q * rest : (q + 1) * rest] for q in range(fold)], axis=0)
    total += jnp.dot(
        left[0:span].astype(jnp.bfloat16), f_ref[full * LANES :, :],
        preferred_element_type=jnp.float32,
    )
    e_ref[...] = total


def apply(h, ft, span, parts):
    depth, width = ft.shape
    blocks = width // BLOCK
    rows = parts[0] * span + parts[3]
    return pl.pallas_call(
        functools.partial(apply_kernel, span, parts),
        out_shape=jax.ShapeDtypeStruct((span, width), jnp.float32),
        grid=(blocks,),
        in_specs=[
            pl.BlockSpec(h.shape, lambda a: (0, 0, 0)),
            pl.BlockSpec((depth, BLOCK), lambda a: (0, a)),
        ],
        out_specs=pl.BlockSpec((span, BLOCK), lambda a: (0, a)),
        scratch_shapes=[pltpu.VMEM((rows * 8, LANES), jnp.float32)],
        compiler_params=pltpu.CompilerParams(vmem_limit_bytes=VMEM),
        name="apply",
    )(h, ft)


def exchange(g):
    return lax.all_to_all(g, "basis", split_axis=0, concat_axis=0, tiled=True)


def shards(factors, orbitals, block_slot, pair_list, pair_owner):
    ndev = lax.axis_size("basis")
    rows, aux, width = factors.shape
    ft = factors.transpose(1, 2, 0).reshape(aux * width, rows)
    xt = orbitals.T
    plans = [plan(hi - lo, aux * width, ndev) for lo, hi in CHUNKS]
    counts = pair_counts(block_slot, pair_list, pair_owner)
    sent = pack(xt, ft, CHUNKS, plans, ndev)
    got = [exchange(g) for g in sent]
    mixed = [mix(counts, g.reshape(ndev, p[4], *g.shape[1:])) for g, p in zip(got, plans)]
    back = [exchange(h.reshape(-1, *h.shape[2:])) for h in mixed]
    parts = [apply(h, ft, hi - lo, p) for h, (lo, hi), p in zip(back, CHUNKS, plans)]
    done = [lax.psum(e, "aux").astype(jnp.bfloat16) for e in parts]
    return jnp.concatenate(done, axis=0).T


def solution(mesh):
    return jax.shard_map(
        shards,
        mesh=mesh,
        in_specs=(P("basis", "aux", None), P("basis", None), P(), P(), P()),
        out_specs=P("basis", None),
        check_vma=False,
    )
```

```python
import functools

import jax
import jax.numpy as jnp
from jax import lax
from jax.experimental import pallas as pl
from jax.experimental.pallas import tpu as pltpu
from jax.sharding import PartitionSpec as P

BLOCK = 256
PAIR_CAP = 64
LANES = 128
VMEM = 56 * 1024 * 1024
NT = (((1,), (1,)), ((), ()))
F32 = jnp.float32
BF16 = jnp.bfloat16


def count_kernel(keep, slot_ref, pairs_ref, owner_ref, low_ref, high_ref, flag_ref):
    nblk = slot_ref.shape[1]
    npair = pairs_ref.shape[1]
    ids = lax.broadcasted_iota(jnp.int32, (nblk, npair), 0)
    owner = owner_ref[...]
    held = jnp.sum((owner == owner_ref[0:1, 0:1]).astype(F32), axis=1, keepdims=True)
    entry = lax.broadcasted_iota(jnp.int32, (1, npair), 1)
    weight = jnp.where(entry == 0, PAIR_CAP + 1.0 - held, 1.0)
    weight = jnp.where(owner >= 0, weight, 0.0)
    one_a = jnp.where(ids == pairs_ref[0:1, :], weight, 0.0).astype(BF16)
    one_b = (ids == pairs_ref[1:2, :]).astype(F32).astype(BF16)
    rows = lax.broadcasted_iota(jnp.int32, (nblk, nblk), 0)
    ndev = nblk // keep
    turned = (rows % ndev) * keep + rows // ndev

    def put(ids, one):
        place = (ids == slot_ref[...]).astype(F32).astype(BF16)
        return jnp.dot(place, one, preferred_element_type=F32).astype(BF16)

    count = lax.dot_general(put(turned, one_a), put(rows, one_b), NT, preferred_element_type=F32)
    count += lax.dot_general(put(turned, one_b), put(rows, one_a), NT, preferred_element_type=F32)
    high = jnp.floor(count * (1.0 / 256.0)) * 256.0
    low_ref[...] = (count - high).astype(BF16)
    high_ref[...] = high.astype(BF16)
    flag_ref[0] = (jnp.max(high) > 0).astype(jnp.int32)


def pair_counts(block_slot, pair_list, pair_owner, keep):
    nblk = block_slot.shape[0]
    square = jax.ShapeDtypeStruct((nblk, nblk), BF16)
    vmem = pl.BlockSpec(memory_space=pltpu.VMEM)
    return pl.pallas_call(
        functools.partial(count_kernel, keep),
        out_shape=(square, square, jax.ShapeDtypeStruct((1,), jnp.int32)),
        in_specs=[vmem] * 3,
        out_specs=(vmem, vmem, pl.BlockSpec(memory_space=pltpu.SMEM)),
        compiler_params=pltpu.CompilerParams(vmem_limit_bytes=VMEM),
        name="pair_counts",
    )(block_slot[None, :], pair_list.T, pair_owner[None, :])


def pack_kernel(per, x_hbm, f_hbm, out_hbm, x_ref, f_ref, out_ref, sems, out_sems):
    span, depth = x_ref.shape[0], f_ref.shape[0]
    full = depth // LANES
    rest = depth - full * LANES
    fold = LANES // rest
    group = -(-span // (fold * 8)) * 8
    step = span // per
    tail = out_ref.shape[0] - full * step
    pairs = f_ref.shape[1] // (2 * BLOCK)

    def fetch(p):
        cols = slice(p * 2 * BLOCK, (p + 1) * 2 * BLOCK)
        return [
            pltpu.make_async_copy(src.at[:, cols], dst.at[:, cols], sems.at[k, p])
            for k, (src, dst) in enumerate(((x_hbm, x_ref), (f_hbm, f_ref)))
        ]

    def send(p):
        rows = slice(p * 2 * per, (p + 1) * 2 * per)
        return pltpu.make_async_copy(out_ref.at[:, rows], out_hbm.at[:, rows], out_sems.at[p])

    for p in range(pairs):
        for copy in fetch(p):
            copy.start()
    for p in range(pairs):
        for copy in fetch(p):
            copy.wait()

        def product(k, lo, hi):
            cols = slice((2 * p + k) * BLOCK, (2 * p + k + 1) * BLOCK)
            return lax.dot_general(
                x_ref[:, cols], f_ref[lo:hi, cols], NT, preferred_element_type=F32
            )

        place = slice(p * 2 * per, (p + 1) * 2 * per)
        for t in range(0, full, 2):
            gs = [product(k, t * LANES, (t + 2) * LANES) for k in range(2)]
            for half in range(2):
                lanes = slice(half * LANES, (half + 1) * LANES)
                rows = [g[:, lanes].reshape(step, per, LANES) for g in gs]
                first = (t + half) * step
                out_ref[first : first + step, place] = jnp.concatenate(rows, axis=1).astype(BF16)
        rows = []
        for k in range(2):
            g = product(k, full * LANES, depth)
            g = jnp.concatenate([g, jnp.zeros((fold * group - span, rest), F32)], axis=0)
            g = jnp.concatenate([g[q * group : (q + 1) * group] for q in range(fold)], axis=1)
            g = jnp.concatenate([g, jnp.zeros((tail * per - group, LANES), F32)], axis=0)
            rows.append(g.reshape(tail, per, LANES))
        out_ref[full * step :, place] = jnp.concatenate(rows, axis=1).astype(BF16)
        send(p).start()
    for p in range(pairs):
        send(p).wait()


def pack(xt, ft, ndev, per):
    depth, width = ft.shape
    blocks = width // BLOCK
    return pl.pallas_call(
        functools.partial(pack_kernel, per),
        out_shape=jax.ShapeDtypeStruct((ndev, blocks * per, LANES), BF16),
        in_specs=[pl.BlockSpec(memory_space=pltpu.HBM)] * 2,
        out_specs=pl.BlockSpec(memory_space=pltpu.HBM),
        scratch_shapes=[
            pltpu.VMEM(xt.shape, BF16),
            pltpu.VMEM(ft.shape, BF16),
            pltpu.VMEM((ndev, blocks * per, LANES), BF16),
            pltpu.SemaphoreType.DMA((2, blocks // 2)),
            pltpu.SemaphoreType.DMA((blocks // 2,)),
        ],
        compiler_params=pltpu.CompilerParams(vmem_limit_bytes=VMEM),
        name="pack",
    )(xt, ft)


def mix_kernel(
    per, flag_ref, low_hbm, high_hbm, g_ref, h_hbm, low_ref, high_ref, stage, turned, h_ref, sems, out_sems
):
    ndev, height, lanes = g_ref.shape
    blocks = height // per
    nblk = low_ref.shape[0]
    pitch = per + 1
    far = blocks * per + 1
    matrices = [
        pltpu.make_async_copy(low_hbm, low_ref, sems.at[0]),
        pltpu.make_async_copy(high_hbm, high_ref, sems.at[1]),
    ]
    for copy in matrices:
        copy.start()
    for c in range(ndev):
        v = g_ref[c].astype(F32)
        for b in range(blocks):
            stage[pl.ds((c * blocks + b) * pitch, per), :] = v[b * per : (b + 1) * per]
    for copy in matrices:
        copy.wait()

    def tiles(use_high):
        for t in range(0, per, 2):
            g = [stage[pl.ds(t + k, nblk, stride=pitch), :].astype(BF16) for k in range(2)]
            g = jnp.concatenate(g, axis=1)
            h = jnp.dot(low_ref[...], g, preferred_element_type=F32)
            if use_high:
                h += jnp.dot(high_ref[...], g, preferred_element_type=F32)
            for k in range(2):
                for a in range(blocks):
                    turned[pl.ds(a * per + t + k, ndev, stride=far), :] = h[
                        a * ndev : (a + 1) * ndev, k * lanes : (k + 1) * lanes
                    ]

    pl.when(flag_ref[0] == 0)(lambda: tiles(False))
    pl.when(flag_ref[0] != 0)(lambda: tiles(True))
    sends = out_sems.shape[0]
    group = ndev // sends

    def send(p):
        cut = slice(p * group, (p + 1) * group)
        return pltpu.make_async_copy(h_ref.at[cut], h_hbm.at[cut], out_sems.at[p])

    for p in range(sends):
        for i in range(p * group, (p + 1) * group):
            h_ref[i] = turned[i * far : i * far + height, :].astype(BF16)
        send(p).start()
    for p in range(sends):
        send(p).wait()


def mix(counts, g, per):
    low, high, flag = counts
    ndev, height, lanes = g.shape
    blocks = height // per
    vmem = pl.BlockSpec(memory_space=pltpu.VMEM)
    hbm = pl.BlockSpec(memory_space=pltpu.HBM)
    return pl.pallas_call(
        functools.partial(mix_kernel, per),
        out_shape=jax.ShapeDtypeStruct(g.shape, BF16),
        in_specs=[
            pl.BlockSpec(memory_space=pltpu.SMEM),
            hbm,
            hbm,
            vmem,
        ],
        out_specs=hbm,
        scratch_shapes=[
            pltpu.VMEM(low.shape, BF16),
            pltpu.VMEM(low.shape, BF16),
            pltpu.VMEM((ndev * blocks * (per + 1), lanes), F32),
            pltpu.VMEM((ndev * (height + 1), lanes), F32),
            pltpu.VMEM(g.shape, BF16),
            pltpu.SemaphoreType.DMA((2,)),
            pltpu.SemaphoreType.DMA((8,)),
        ],
        compiler_params=pltpu.CompilerParams(vmem_limit_bytes=VMEM),
        name="mix",
    )(flag, low, high, g)


def apply_kernel(per, me_ref, h_ref, f_hbm, *refs):
    outs, f_ref, sems = refs[:-2], *refs[-2:]
    ndev, height, lanes = h_ref.shape
    span = outs[0].shape[0]
    depth = f_hbm.shape[0]
    aux, _, width = f_ref.shape
    keep = width // BLOCK
    full = depth // LANES
    rest = depth - full * LANES
    fold = LANES // rest
    group = -(-span // (fold * 8)) * 8
    step = span // per

    def fetch(d):
        start = pl.multiple_of(lax.rem(me_ref[0] + d, aux) * width, width)
        return pltpu.make_async_copy(f_hbm.at[:, pl.ds(start, width)], f_ref.at[d], sems.at[d])

    order = list(range(1, aux)) + [0]
    for d in order:
        fetch(d).start()
    for d in order:
        fetch(d).wait()
        chunk = keep * per
        first = pl.multiple_of(lax.rem(me_ref[0] + d, aux) * chunk, chunk)

        def take(lo, hi):
            return h_ref[lo:hi, pl.ds(first, chunk)].astype(F32)

        tiles = [take(t * step, (t + 1) * step) for t in range(full)]
        tail = take(full * step, ndev)
        for a in range(keep):
            rows = slice(a * per, (a + 1) * per)
            left = [v[:, rows].reshape(span, lanes).astype(BF16) for v in tiles]
            last = tail[:, rows].reshape(-1, lanes)[:group]
            last = [last[:, q * rest : (q + 1) * rest] for q in range(fold)]
            last = jnp.concatenate(last, axis=0)[:span].astype(BF16)
            left = jnp.concatenate(left + [last], axis=1)
            cols = slice(a * BLOCK, (a + 1) * BLOCK)
            total = jnp.dot(left, f_ref[d, :, cols], preferred_element_type=F32)
            out = outs[a * aux + d]
            out[...] = total.astype(out.dtype)


def apply(me, h, ft, span, per, aux):
    depth, rows = ft.shape
    width = rows // aux
    vmem = pl.BlockSpec(memory_space=pltpu.VMEM)
    return pl.pallas_call(
        functools.partial(apply_kernel, per),
        out_shape=[
            pltpu.VMEM((span, BLOCK), BF16 if d else F32)
            for a in range(width // BLOCK)
            for d in range(aux)
        ],
        in_specs=[
            pl.BlockSpec(memory_space=pltpu.SMEM),
            vmem,
            pl.BlockSpec(memory_space=pltpu.HBM),
        ],
        out_specs=[vmem] * (rows // BLOCK),
        scratch_shapes=[
            pltpu.VMEM((aux, depth, width), BF16),
            pltpu.SemaphoreType.DMA((aux,)),
        ],
        compiler_params=pltpu.CompilerParams(vmem_limit_bytes=VMEM),
        name="apply",
    )(me, h, ft)


def place_kernel(aux, me_ref, *refs):
    pieces, out_ref = refs[:-1], refs[-1]
    keep = len(pieces) // aux
    for d in range(aux):
        h = lax.rem(me_ref[0] + aux - d, aux)
        for a in range(keep):
            start = pl.multiple_of((h * keep + a) * BLOCK, BLOCK)
            out_ref[:, pl.ds(start, BLOCK)] = pieces[a * aux + d][...]


def place(me, pieces, aux):
    span, width = pieces[0].shape
    vmem = pl.BlockSpec(memory_space=pltpu.VMEM)
    return pl.pallas_call(
        functools.partial(place_kernel, aux),
        out_shape=jax.ShapeDtypeStruct((span, width * len(pieces)), BF16),
        in_specs=[pl.BlockSpec(memory_space=pltpu.SMEM)] + [vmem] * len(pieces),
        out_specs=vmem,
        compiler_params=pltpu.CompilerParams(vmem_limit_bytes=VMEM),
        name="place",
    )(me, *pieces)


def exchange(v):
    v = lax.all_to_all(v, "basis", split_axis=0, concat_axis=0, tiled=True)
    return pltpu.with_memory_space_constraint(v, pltpu.VMEM)


def shards(factors, orbitals, block_slot, pair_list, pair_owner):
    ndev, aux = lax.axis_size("basis"), lax.axis_size("aux")
    me = lax.axis_index("aux").astype(jnp.int32)
    rows, aux_dev, width = factors.shape
    ft = factors.transpose(1, 2, 0).reshape(aux_dev * width, rows)
    xt = orbitals.T
    blocks = rows // BLOCK
    per = -(-(aux_dev * width * width) // (LANES * ndev * 8)) * 8
    got = exchange(pack(xt, ft, ndev, per))
    counts = pair_counts(block_slot, pair_list, pair_owner, blocks)
    back = exchange(mix(counts, got, per))
    parts = apply(me[None], back, ft, width, per, aux)

    def turn(v, d, last):
        v = lax.ppermute(v, "aux", [(k, (k + d) % aux) for k in range(aux)])
        return pltpu.with_memory_space_constraint(v, pltpu.VMEM) if last else v

    pieces = []
    for a in range(blocks // aux):
        total = parts[a * aux]
        for d in range(1, aux):
            total += turn(parts[a * aux + d], d, False).astype(F32)
        total = total.astype(BF16)
        pieces += [turn(total, d, True) if d else total for d in range(aux)]
    return place(me[None], pieces, aux).T


def solution(mesh):
    return jax.shard_map(
        shards,
        mesh=mesh,
        in_specs=(P("basis", "aux", None), P("basis", None), P(), P(), P()),
        out_specs=P("basis", None),
        check_vma=False,
    )
```

```python
import functools

import jax
import jax.numpy as jnp
from jax import lax
from jax.experimental import pallas as pl
from jax.experimental.pallas import tpu as pltpu
from jax.sharding import PartitionSpec as P

BLOCK = 256
PAIR_CAP = 64
LANES = 128
VMEM = 56 * 1024 * 1024
NT = (((1,), (1,)), ((), ()))
F32 = jnp.float32
BF16 = jnp.bfloat16


def count_kernel(keep, slot_ref, pairs_ref, owner_ref, low_ref, high_ref, flag_ref):
    nblk = slot_ref.shape[1]
    npair = pairs_ref.shape[1]
    ids = lax.broadcasted_iota(jnp.int32, (nblk, npair), 0)
    owner = owner_ref[...]
    held = jnp.sum((owner == owner_ref[0:1, 0:1]).astype(F32), axis=1, keepdims=True)
    entry = lax.broadcasted_iota(jnp.int32, (1, npair), 1)
    weight = jnp.where(entry == 0, PAIR_CAP + 1.0 - held, 1.0)
    weight = jnp.where(owner >= 0, weight, 0.0)
    one_a = jnp.where(ids == pairs_ref[0:1, :], weight, 0.0).astype(BF16)
    one_b = (ids == pairs_ref[1:2, :]).astype(F32).astype(BF16)
    rows = lax.broadcasted_iota(jnp.int32, (nblk, nblk), 0)
    ndev = nblk // keep
    turned = (rows % ndev) * keep + rows // ndev

    def put(ids, one):
        place = (ids == slot_ref[...]).astype(F32).astype(BF16)
        return jnp.dot(place, one, preferred_element_type=F32).astype(BF16)

    count = lax.dot_general(put(turned, one_a), put(rows, one_b), NT, preferred_element_type=F32)
    count += lax.dot_general(put(turned, one_b), put(rows, one_a), NT, preferred_element_type=F32)
    high = jnp.floor(count * (1.0 / 256.0)) * 256.0
    low_ref[...] = (count - high).astype(BF16)
    high_ref[...] = high.astype(BF16)
    flag_ref[0] = (jnp.max(high) > 0).astype(jnp.int32)


def pair_counts(block_slot, pair_list, pair_owner, keep):
    nblk = block_slot.shape[0]
    square = jax.ShapeDtypeStruct((nblk, nblk), BF16)
    vmem = pl.BlockSpec(memory_space=pltpu.VMEM)
    return pl.pallas_call(
        functools.partial(count_kernel, keep),
        out_shape=(square, square, jax.ShapeDtypeStruct((1,), jnp.int32)),
        in_specs=[vmem] * 3,
        out_specs=(vmem, vmem, pl.BlockSpec(memory_space=pltpu.SMEM)),
        compiler_params=pltpu.CompilerParams(vmem_limit_bytes=VMEM),
        name="pair_counts",
    )(block_slot[None, :], pair_list.T, pair_owner[None, :])


def pack_kernel(per, me_ref, x_hbm, f_hbm, out_hbm, *refs):
    f_out, (x_ref, f_ref, out_ref, sems, out_sems, f_sems) = refs[:-6], refs[-6:]
    aux, span, width = x_ref.shape
    depth = f_ref.shape[1]
    keep = width // BLOCK
    full = depth // LANES
    rest = depth - full * LANES
    fold = LANES // rest
    group = -(-span // (fold * 8)) * 8
    step = span // per
    tail = out_ref.shape[0] - full * step

    def at(d, size):
        return pl.ds(pl.multiple_of(lax.rem(me_ref[0] + d, aux) * size, size), size)

    def fetch(d):
        return [
            pltpu.make_async_copy(src.at[:, at(d, width)], dst.at[d], sems.at[k, d])
            for k, (src, dst) in enumerate(((x_hbm, x_ref), (f_hbm, f_ref)))
        ]

    def send(d):
        rows = at(d, keep * per)
        copies = [pltpu.make_async_copy(out_ref.at[:, rows], out_hbm.at[:, rows], out_sems.at[d])]
        for a in range(keep if d else 0):
            k = (d - 1) * keep + a
            cols = slice(a * BLOCK, (a + 1) * BLOCK)
            copies.append(pltpu.make_async_copy(f_ref.at[d, :, cols], f_out[k], f_sems.at[k]))
        return copies

    order = list(range(1, aux)) + [0]
    for d in order:
        for copy in fetch(d):
            copy.start()
    for d in order:
        for copy in fetch(d):
            copy.wait()

        def product(k, lo, hi):
            cols = slice(k * BLOCK, (k + 1) * BLOCK)
            return lax.dot_general(
                x_ref[d, :, cols], f_ref[d, lo:hi, cols], NT, preferred_element_type=F32
            )

        place = at(d, keep * per)
        for t in range(0, full, 2):
            gs = [product(k, t * LANES, (t + 2) * LANES) for k in range(keep)]
            for half in range(2):
                lanes = slice(half * LANES, (half + 1) * LANES)
                rows = [g[:, lanes].reshape(step, per, LANES) for g in gs]
                first = (t + half) * step
                out_ref[first : first + step, place] = jnp.concatenate(rows, axis=1).astype(BF16)
        rows = []
        for k in range(keep):
            g = product(k, full * LANES, depth)
            g = jnp.concatenate([g, jnp.zeros((fold * group - span, rest), F32)], axis=0)
            g = jnp.concatenate([g[q * group : (q + 1) * group] for q in range(fold)], axis=1)
            g = jnp.concatenate([g, jnp.zeros((tail * per - group, LANES), F32)], axis=0)
            rows.append(g.reshape(tail, per, LANES))
        out_ref[full * step :, place] = jnp.concatenate(rows, axis=1).astype(BF16)
        for copy in send(d):
            copy.start()
    for d in order:
        for copy in send(d):
            copy.wait()


def pack(me, xt, ft, ndev, aux, per):
    depth, rows = ft.shape
    blocks = rows // BLOCK
    width = rows // aux
    count = (aux - 1) * (width // BLOCK)
    hbm = pl.BlockSpec(memory_space=pltpu.HBM)
    shape = jax.ShapeDtypeStruct((ndev, blocks * per, LANES), BF16)
    piece = jax.ShapeDtypeStruct((depth, BLOCK), BF16)
    return pl.pallas_call(
        functools.partial(pack_kernel, per),
        out_shape=[shape] + [piece] * count,
        in_specs=[pl.BlockSpec(memory_space=pltpu.SMEM), hbm, hbm],
        out_specs=[hbm] * (1 + count),
        scratch_shapes=[
            pltpu.VMEM((aux, xt.shape[0], width), BF16),
            pltpu.VMEM((aux, depth, width), BF16),
            pltpu.VMEM(shape.shape, BF16),
            pltpu.SemaphoreType.DMA((2, aux)),
            pltpu.SemaphoreType.DMA((aux,)),
            pltpu.SemaphoreType.DMA((count,)),
        ],
        compiler_params=pltpu.CompilerParams(vmem_limit_bytes=VMEM),
        name="pack",
    )(me, xt, ft)


def mix_kernel(
    per, flag_ref, low_hbm, high_hbm, g_ref, h_hbm, low_ref, high_ref, stage, turned, h_ref, sems, out_sems
):
    ndev, height, lanes = g_ref.shape
    blocks = height // per
    nblk = low_ref.shape[0]
    pitch = per + 1
    far = blocks * per + 1
    matrices = [
        pltpu.make_async_copy(low_hbm, low_ref, sems.at[0]),
        pltpu.make_async_copy(high_hbm, high_ref, sems.at[1]),
    ]
    for copy in matrices:
        copy.start()
    for c in range(ndev):
        v = g_ref[c].astype(F32)
        for b in range(blocks):
            stage[pl.ds((c * blocks + b) * pitch, per), :] = v[b * per : (b + 1) * per]
    for copy in matrices:
        copy.wait()

    def tiles(use_high):
        for t in range(0, per, 2):
            g = [stage[pl.ds(t + k, nblk, stride=pitch), :].astype(BF16) for k in range(2)]
            g = jnp.concatenate(g, axis=1)
            h = jnp.dot(low_ref[...], g, preferred_element_type=F32)
            if use_high:
                h += jnp.dot(high_ref[...], g, preferred_element_type=F32)
            for k in range(2):
                for a in range(blocks):
                    turned[pl.ds(a * per + t + k, ndev, stride=far), :] = h[
                        a * ndev : (a + 1) * ndev, k * lanes : (k + 1) * lanes
                    ]

    pl.when(flag_ref[0] == 0)(lambda: tiles(False))
    pl.when(flag_ref[0] != 0)(lambda: tiles(True))
    sends = out_sems.shape[0]
    group = ndev // sends

    def send(p):
        cut = slice(p * group, (p + 1) * group)
        return pltpu.make_async_copy(h_ref.at[cut], h_hbm.at[cut], out_sems.at[p])

    for p in range(sends):
        for i in range(p * group, (p + 1) * group):
            h_ref[i] = turned[i * far : i * far + height, :].astype(BF16)
        send(p).start()
    for p in range(sends):
        send(p).wait()


def mix(counts, g, per):
    low, high, flag = counts
    ndev, height, lanes = g.shape
    blocks = height // per
    vmem = pl.BlockSpec(memory_space=pltpu.VMEM)
    hbm = pl.BlockSpec(memory_space=pltpu.HBM)
    return pl.pallas_call(
        functools.partial(mix_kernel, per),
        out_shape=jax.ShapeDtypeStruct(g.shape, BF16),
        in_specs=[
            pl.BlockSpec(memory_space=pltpu.SMEM),
            hbm,
            hbm,
            vmem,
        ],
        out_specs=hbm,
        scratch_shapes=[
            pltpu.VMEM(low.shape, BF16),
            pltpu.VMEM(low.shape, BF16),
            pltpu.VMEM((ndev * blocks * (per + 1), lanes), F32),
            pltpu.VMEM((ndev * (height + 1), lanes), F32),
            pltpu.VMEM(g.shape, BF16),
            pltpu.SemaphoreType.DMA((2,)),
            pltpu.SemaphoreType.DMA((8,)),
        ],
        compiler_params=pltpu.CompilerParams(vmem_limit_bytes=VMEM),
        name="mix",
    )(flag, low, high, g)


def apply_kernel(per, a, count, me_ref, h_ref, *refs):
    f_hbm, e_ref, f_ref, f_sems = refs[:count], *refs[count:]
    ndev, aux, height, lanes = h_ref.shape
    span = e_ref.shape[0]
    depth = f_ref.shape[1]
    full = depth // LANES
    rest = depth - full * LANES
    fold = LANES // rest
    group = -(-span // (fold * 8)) * 8
    step = span // per
    rows = slice(a * per, (a + 1) * per)
    start = pl.multiple_of((me_ref[0] * (height // per) + a) * BLOCK, BLOCK)
    sources = [f_hbm[0].at[:, pl.ds(start, BLOCK)], *f_hbm[1:]]
    copies = [pltpu.make_async_copy(sources[d], f_ref.at[d], f_sems.at[d]) for d in range(aux)]
    for copy in copies:
        copy.start()
    total = jnp.zeros((span, BLOCK), F32)
    for d in range(aux):
        h = lax.rem(me_ref[0] + aux - d, aux)

        def take(lo, hi):
            v = h_ref[lo:hi, pl.ds(h, 1)].reshape(hi - lo, height, lanes).astype(F32)
            return v[:, rows].reshape(-1, lanes)

        left = [take(t * step, (t + 1) * step).astype(BF16) for t in range(full)]
        last = take(full * step, ndev)[:group]
        last = [last[:, q * rest : (q + 1) * rest] for q in range(fold)]
        last = jnp.concatenate(last, axis=0)[:span].astype(BF16)
        left = jnp.concatenate(left + [last], axis=1)
        copies[d].wait()
        total += jnp.dot(left, f_ref[d], preferred_element_type=F32)
    e_ref[...] = total.astype(BF16)


def apply(me, h, fs, spaces, a, span, per):
    depth, width = fs[1].shape
    aux = h.shape[1]
    vmem = pl.BlockSpec(memory_space=pltpu.VMEM)
    return pl.pallas_call(
        functools.partial(apply_kernel, per, a, len(fs)),
        out_shape=pltpu.VMEM((span, width), BF16),
        in_specs=[pl.BlockSpec(memory_space=pltpu.SMEM), vmem]
        + [pl.BlockSpec(memory_space=space) for space in spaces],
        out_specs=vmem,
        scratch_shapes=[
            pltpu.VMEM((aux, depth, width), BF16),
            pltpu.SemaphoreType.DMA((aux,)),
        ],
        compiler_params=pltpu.CompilerParams(vmem_limit_bytes=VMEM),
        name="apply",
    )(me, h, *fs)


def place_kernel(aux, me_ref, *refs):
    pieces, out_hbm, sems = refs[:-2], refs[-2], refs[-1]
    keep = len(pieces) // aux
    copies = []
    for k, piece in enumerate(pieces):
        h = lax.rem(me_ref[0] + aux - k % aux, aux)
        start = pl.multiple_of((h * keep + k // aux) * BLOCK, BLOCK)
        copies.append(pltpu.make_async_copy(piece, out_hbm.at[:, pl.ds(start, BLOCK)], sems.at[k]))
    for copy in copies:
        copy.start()
    for copy in copies:
        copy.wait()


def place(me, pieces, aux):
    span, width = pieces[0].shape
    vmem = pl.BlockSpec(memory_space=pltpu.VMEM)
    return pl.pallas_call(
        functools.partial(place_kernel, aux),
        out_shape=jax.ShapeDtypeStruct((span, width * len(pieces)), BF16),
        in_specs=[pl.BlockSpec(memory_space=pltpu.SMEM)] + [vmem] * len(pieces),
        out_specs=pl.BlockSpec(memory_space=pltpu.HBM),
        scratch_shapes=[pltpu.SemaphoreType.DMA((len(pieces),))],
        compiler_params=pltpu.CompilerParams(vmem_limit_bytes=VMEM),
        name="place",
    )(me, *pieces)


def shards(factors, orbitals, block_slot, pair_list, pair_owner):
    ndev, aux = lax.axis_size("basis"), lax.axis_size("aux")
    me = lax.axis_index("aux").astype(jnp.int32)
    rows, aux_dev, width = factors.shape
    ft = factors.transpose(1, 2, 0).reshape(aux_dev * width, rows)
    xt = orbitals.T
    blocks = rows // BLOCK
    keep = blocks // aux
    per = -(-(aux_dev * width * width) // (LANES * ndev * 8)) * 8

    def turn(v, d):
        return lax.ppermute(v, "aux", [(k, (k + d) % aux) for k in range(aux)])

    sent, *pieces = pack(me[None], xt, ft, ndev, aux, per)
    got = lax.all_to_all(sent, "basis", split_axis=0, concat_axis=0, tiled=True)
    counts = pair_counts(block_slot, pair_list, pair_owner, blocks)
    far = aux // 2
    fs = {(d, a): turn(pieces[(d - 1) * keep + a], d) for d in range(1, aux) for a in range(keep)}
    early = {k: v for k, v in fs.items() if k != (far, 0)}
    got, early = lax.optimization_barrier((got, early))
    fs.update(early)
    spaces = {k: pltpu.HBM if k in early else pltpu.VMEM for k in fs}
    fs = {k: pltpu.with_memory_space_constraint(v, spaces[k]) for k, v in fs.items()}
    fs.update({(0, a): ft for a in range(keep)})
    got = pltpu.with_memory_space_constraint(got, pltpu.VMEM)
    mixed = mix(counts, got, per)
    mixed = mixed.reshape(ndev * aux, -1, LANES)
    back = lax.all_to_all(mixed, ("basis", "aux"), split_axis=0, concat_axis=0, tiled=True)
    back = back.reshape(ndev, aux, *back.shape[1:])
    back = pltpu.with_memory_space_constraint(back, pltpu.VMEM)
    done = {}
    for a in range(keep):
        kinds = [spaces.get((d, a), pltpu.HBM) for d in range(aux)]
        mine = apply(me[None], back, [fs[d, a] for d in range(aux)], kinds, a, width, per)
        for d in range(1, aux):
            done[d, a] = pltpu.with_memory_space_constraint(turn(mine, d), pltpu.VMEM)
        done[0, a] = mine
    done = [done[d, a] for a in range(keep) for d in range(aux)]
    return place(me[None], done, aux).T


def solution(mesh):
    return jax.shard_map(
        shards,
        mesh=mesh,
        in_specs=(P("basis", "aux", None), P("basis", None), P(), P(), P()),
        out_specs=P("basis", None),
        check_vma=False,
    )
```

```python
import functools

import jax
import jax.numpy as jnp
from jax import lax
from jax.experimental import pallas as pl
from jax.experimental.pallas import tpu as pltpu
from jax.sharding import PartitionSpec as P

BLOCK = 256
PAIR_CAP = 64
LANES = 128
VMEM = 56 * 1024 * 1024
NT = (((1,), (1,)), ((), ()))
F32 = jnp.float32
BF16 = jnp.bfloat16


def count_kernel(keep, slot_ref, pairs_ref, owner_ref, low_ref, high_ref, flag_ref):
    nblk = slot_ref.shape[1]
    npair = pairs_ref.shape[1]
    ids = lax.broadcasted_iota(jnp.int32, (nblk, npair), 0)
    owner = owner_ref[...]
    held = jnp.sum((owner == owner_ref[0:1, 0:1]).astype(F32), axis=1, keepdims=True)
    entry = lax.broadcasted_iota(jnp.int32, (1, npair), 1)
    weight = jnp.where(entry == 0, PAIR_CAP + 1.0 - held, 1.0)
    weight = jnp.where(owner >= 0, weight, 0.0)
    one_a = jnp.where(ids == pairs_ref[0:1, :], weight, 0.0).astype(BF16)
    one_b = (ids == pairs_ref[1:2, :]).astype(F32).astype(BF16)
    rows = lax.broadcasted_iota(jnp.int32, (nblk, nblk), 0)
    ndev = nblk // keep
    turned = (rows % ndev) * keep + rows // ndev

    def put(ids, one):
        place = (ids == slot_ref[...]).astype(F32).astype(BF16)
        return jnp.dot(place, one, preferred_element_type=F32).astype(BF16)

    count = lax.dot_general(put(turned, one_a), put(rows, one_b), NT, preferred_element_type=F32)
    count += lax.dot_general(put(turned, one_b), put(rows, one_a), NT, preferred_element_type=F32)
    high = jnp.floor(count * (1.0 / 256.0)) * 256.0
    low_ref[...] = (count - high).astype(BF16)
    high_ref[...] = high.astype(BF16)
    flag_ref[0] = (jnp.max(high) > 0).astype(jnp.int32)


def pair_counts(block_slot, pair_list, pair_owner, keep):
    nblk = block_slot.shape[0]
    square = jax.ShapeDtypeStruct((nblk, nblk), BF16)
    vmem = pl.BlockSpec(memory_space=pltpu.VMEM)
    return pl.pallas_call(
        functools.partial(count_kernel, keep),
        out_shape=(square, square, jax.ShapeDtypeStruct((1,), jnp.int32)),
        in_specs=[vmem] * 3,
        out_specs=(vmem, vmem, pl.BlockSpec(memory_space=pltpu.SMEM)),
        compiler_params=pltpu.CompilerParams(vmem_limit_bytes=VMEM),
        name="pair_counts",
    )(block_slot[None, :], pair_list.T, pair_owner[None, :])


def pack_kernel(per, me_ref, x_hbm, f_hbm, out_hbm, *refs):
    f_out, (x_ref, f_ref, out_ref, sems, out_sems, f_sems) = refs[:-6], refs[-6:]
    aux, span, width = x_ref.shape
    depth = f_ref.shape[1]
    keep = width // BLOCK
    full = depth // LANES
    rest = depth - full * LANES
    fold = LANES // rest
    group = -(-span // (fold * 8)) * 8
    step = span // per
    tail = out_ref.shape[0] - full * step

    def at(d, size):
        return pl.ds(pl.multiple_of(lax.rem(me_ref[0] + d, aux) * size, size), size)

    def fetch(d):
        return [
            pltpu.make_async_copy(src.at[:, at(d, width)], dst.at[d], sems.at[k, d])
            for k, (src, dst) in enumerate(((x_hbm, x_ref), (f_hbm, f_ref)))
        ]

    def send(d):
        rows = at(d, keep * per)
        return pltpu.make_async_copy(out_ref.at[:, rows], out_hbm.at[:, rows], out_sems.at[d])

    def pass_on(d):
        copies = []
        for a in range(keep if d else 0):
            k = (d - 1) * keep + a
            cols = slice(a * BLOCK, (a + 1) * BLOCK)
            copies.append(pltpu.make_async_copy(f_ref.at[d, :, cols], f_out[k], f_sems.at[k]))
        return copies

    order = list(range(1, aux)) + [0]
    for d in order:
        for copy in fetch(d):
            copy.start()
    for d in order:
        for copy in fetch(d):
            copy.wait()
        for copy in pass_on(d):
            copy.start()

        def product(k, lo, hi):
            cols = slice(k * BLOCK, (k + 1) * BLOCK)
            return lax.dot_general(
                x_ref[d, :, cols], f_ref[d, lo:hi, cols], NT, preferred_element_type=F32
            )

        place = at(d, keep * per)
        for t in range(0, full, 2):
            gs = [product(k, t * LANES, (t + 2) * LANES) for k in range(keep)]
            for half in range(2):
                lanes = slice(half * LANES, (half + 1) * LANES)
                rows = [g[:, lanes].reshape(step, per, LANES) for g in gs]
                first = (t + half) * step
                out_ref[first : first + step, place] = jnp.concatenate(rows, axis=1).astype(BF16)
        rows = []
        for k in range(keep):
            g = product(k, full * LANES, depth)
            g = jnp.concatenate([g, jnp.zeros((fold * group - span, rest), F32)], axis=0)
            g = jnp.concatenate([g[q * group : (q + 1) * group] for q in range(fold)], axis=1)
            g = jnp.concatenate([g, jnp.zeros((tail * per - group, LANES), F32)], axis=0)
            rows.append(g.reshape(tail, per, LANES))
        out_ref[full * step :, place] = jnp.concatenate(rows, axis=1).astype(BF16)
        send(d).start()
    for d in order:
        for copy in (*pass_on(d), send(d)):
            copy.wait()


def pack(me, xt, ft, ndev, aux, per):
    depth, rows = ft.shape
    blocks = rows // BLOCK
    width = rows // aux
    count = (aux - 1) * (width // BLOCK)
    hbm = pl.BlockSpec(memory_space=pltpu.HBM)
    shape = jax.ShapeDtypeStruct((ndev, blocks * per, LANES), BF16)
    piece = jax.ShapeDtypeStruct((depth, BLOCK), BF16)
    return pl.pallas_call(
        functools.partial(pack_kernel, per),
        out_shape=[shape] + [piece] * count,
        in_specs=[pl.BlockSpec(memory_space=pltpu.SMEM), hbm, hbm],
        out_specs=[hbm] * (1 + count),
        scratch_shapes=[
            pltpu.VMEM((aux, xt.shape[0], width), BF16),
            pltpu.VMEM((aux, depth, width), BF16),
            pltpu.VMEM(shape.shape, BF16),
            pltpu.SemaphoreType.DMA((2, aux)),
            pltpu.SemaphoreType.DMA((aux,)),
            pltpu.SemaphoreType.DMA((count,)),
        ],
        compiler_params=pltpu.CompilerParams(vmem_limit_bytes=VMEM),
        name="pack",
    )(me, xt, ft)


def mix_kernel(
    per, flag_ref, low_hbm, high_hbm, g_ref, h_hbm, low_ref, high_ref, stage, turned, h_ref, sems, out_sems
):
    ndev, height, lanes = g_ref.shape
    blocks = height // per
    nblk = low_ref.shape[0]
    pitch = per + 1
    far = blocks * per + 1
    matrices = [
        pltpu.make_async_copy(low_hbm, low_ref, sems.at[0]),
        pltpu.make_async_copy(high_hbm, high_ref, sems.at[1]),
    ]
    for copy in matrices:
        copy.start()
    for c in range(ndev):
        v = g_ref[c].astype(F32)
        for b in range(blocks):
            stage[pl.ds((c * blocks + b) * pitch, per), :] = v[b * per : (b + 1) * per]
    for copy in matrices:
        copy.wait()

    def tiles(use_high):
        for t in range(0, per, 2):
            g = [stage[pl.ds(t + k, nblk, stride=pitch), :].astype(BF16) for k in range(2)]
            g = jnp.concatenate(g, axis=1)
            h = jnp.dot(low_ref[...], g, preferred_element_type=F32)
            if use_high:
                h += jnp.dot(high_ref[...], g, preferred_element_type=F32)
            for k in range(2):
                for a in range(blocks):
                    turned[pl.ds(a * per + t + k, ndev, stride=far), :] = h[
                        a * ndev : (a + 1) * ndev, k * lanes : (k + 1) * lanes
                    ]

    pl.when(flag_ref[0] == 0)(lambda: tiles(False))
    pl.when(flag_ref[0] != 0)(lambda: tiles(True))
    sends = out_sems.shape[0]
    group = ndev // sends

    def send(p):
        cut = slice(p * group, (p + 1) * group)
        return pltpu.make_async_copy(h_ref.at[cut], h_hbm.at[cut], out_sems.at[p])

    for p in range(sends):
        for i in range(p * group, (p + 1) * group):
            h_ref[i] = turned[i * far : i * far + height, :].astype(BF16)
        send(p).start()
    for p in range(sends):
        send(p).wait()


def mix(counts, g, per):
    low, high, flag = counts
    ndev, height, lanes = g.shape
    blocks = height // per
    vmem = pl.BlockSpec(memory_space=pltpu.VMEM)
    hbm = pl.BlockSpec(memory_space=pltpu.HBM)
    return pl.pallas_call(
        functools.partial(mix_kernel, per),
        out_shape=jax.ShapeDtypeStruct(g.shape, BF16),
        in_specs=[
            pl.BlockSpec(memory_space=pltpu.SMEM),
            hbm,
            hbm,
            vmem,
        ],
        out_specs=hbm,
        scratch_shapes=[
            pltpu.VMEM(low.shape, BF16),
            pltpu.VMEM(low.shape, BF16),
            pltpu.VMEM((ndev * blocks * (per + 1), lanes), F32),
            pltpu.VMEM((ndev * (height + 1), lanes), F32),
            pltpu.VMEM(g.shape, BF16),
            pltpu.SemaphoreType.DMA((2,)),
            pltpu.SemaphoreType.DMA((8,)),
        ],
        compiler_params=pltpu.CompilerParams(vmem_limit_bytes=VMEM),
        name="mix",
    )(flag, low, high, g)


def apply_kernel(per, a, count, me_ref, h_ref, *refs):
    f_hbm, e_ref, f_ref, f_sems = refs[:count], *refs[count:]
    ndev, aux, height, lanes = h_ref.shape
    span = e_ref.shape[0]
    depth = f_ref.shape[1]
    full = depth // LANES
    rest = depth - full * LANES
    fold = LANES // rest
    group = -(-span // (fold * 8)) * 8
    step = span // per
    rows = slice(a * per, (a + 1) * per)
    start = pl.multiple_of((me_ref[0] * (height // per) + a) * BLOCK, BLOCK)
    sources = [f_hbm[0].at[:, pl.ds(start, BLOCK)], *f_hbm[1:]]
    copies = [pltpu.make_async_copy(sources[d], f_ref.at[d], f_sems.at[d]) for d in range(aux)]
    for copy in copies:
        copy.start()
    total = jnp.zeros((span, BLOCK), F32)
    for d in range(aux):
        h = lax.rem(me_ref[0] + aux - d, aux)

        def take(lo, hi):
            v = h_ref[lo:hi, pl.ds(h, 1)].reshape(hi - lo, height, lanes).astype(F32)
            return v[:, rows].reshape(-1, lanes)

        left = [take(t * step, (t + 1) * step).astype(BF16) for t in range(full)]
        last = take(full * step, ndev)[:group]
        last = [last[:, q * rest : (q + 1) * rest] for q in range(fold)]
        last = jnp.concatenate(last, axis=0)[:span].astype(BF16)
        left = jnp.concatenate(left + [last], axis=1)
        copies[d].wait()
        total += jnp.dot(left, f_ref[d], preferred_element_type=F32)
    e_ref[...] = total.astype(BF16)


def apply(me, h, fs, spaces, a, span, per):
    depth, width = fs[1].shape
    aux = h.shape[1]
    vmem = pl.BlockSpec(memory_space=pltpu.VMEM)
    return pl.pallas_call(
        functools.partial(apply_kernel, per, a, len(fs)),
        out_shape=pltpu.VMEM((span, width), BF16),
        in_specs=[pl.BlockSpec(memory_space=pltpu.SMEM), vmem]
        + [pl.BlockSpec(memory_space=space) for space in spaces],
        out_specs=vmem,
        scratch_shapes=[
            pltpu.VMEM((aux, depth, width), BF16),
            pltpu.SemaphoreType.DMA((aux,)),
        ],
        compiler_params=pltpu.CompilerParams(vmem_limit_bytes=VMEM),
        name="apply",
    )(me, h, *fs)


def place_kernel(aux, me_ref, *refs):
    pieces, out_hbm, sems = refs[:-2], refs[-2], refs[-1]
    keep = len(pieces) // aux
    copies = []
    for k, piece in enumerate(pieces):
        h = lax.rem(me_ref[0] + aux - k % aux, aux)
        start = pl.multiple_of((h * keep + k // aux) * BLOCK, BLOCK)
        copies.append(pltpu.make_async_copy(piece, out_hbm.at[:, pl.ds(start, BLOCK)], sems.at[k]))
    for copy in copies:
        copy.start()
    for copy in copies:
        copy.wait()


def place(me, pieces, aux):
    span, width = pieces[0].shape
    vmem = pl.BlockSpec(memory_space=pltpu.VMEM)
    return pl.pallas_call(
        functools.partial(place_kernel, aux),
        out_shape=jax.ShapeDtypeStruct((span, width * len(pieces)), BF16),
        in_specs=[pl.BlockSpec(memory_space=pltpu.SMEM)] + [vmem] * len(pieces),
        out_specs=pl.BlockSpec(memory_space=pltpu.HBM),
        scratch_shapes=[pltpu.SemaphoreType.DMA((len(pieces),))],
        compiler_params=pltpu.CompilerParams(vmem_limit_bytes=VMEM),
        name="place",
    )(me, *pieces)


def shards(factors, orbitals, block_slot, pair_list, pair_owner):
    ndev, aux = lax.axis_size("basis"), lax.axis_size("aux")
    me = lax.axis_index("aux").astype(jnp.int32)
    rows, aux_dev, width = factors.shape
    ft = factors.transpose(1, 2, 0).reshape(aux_dev * width, rows)
    xt = orbitals.T
    blocks = rows // BLOCK
    keep = blocks // aux
    per = -(-(aux_dev * width * width) // (LANES * ndev * 8)) * 8

    def turn(v, d):
        return lax.ppermute(v, "aux", [(k, (k + d) % aux) for k in range(aux)])

    sent, *pieces = pack(me[None], xt, ft, ndev, aux, per)
    got = lax.all_to_all(sent, "basis", split_axis=0, concat_axis=0, tiled=True)
    counts = pair_counts(block_slot, pair_list, pair_owner, blocks)
    far = aux // 2
    fs = {(d, a): turn(pieces[(d - 1) * keep + a], d) for d in range(1, aux) for a in range(keep)}
    early = {k: v for k, v in fs.items() if k != (far, 0)}
    got, early = lax.optimization_barrier((got, early))
    fs.update(early)
    spaces = {k: pltpu.HBM if k in early else pltpu.VMEM for k in fs}
    fs = {k: pltpu.with_memory_space_constraint(v, spaces[k]) for k, v in fs.items()}
    fs.update({(0, a): ft for a in range(keep)})
    got = pltpu.with_memory_space_constraint(got, pltpu.VMEM)
    mixed = mix(counts, got, per)
    mixed = mixed.reshape(ndev * aux, -1, LANES)
    back = lax.all_to_all(mixed, ("basis", "aux"), split_axis=0, concat_axis=0, tiled=True)
    back = back.reshape(ndev, aux, *back.shape[1:])
    back = pltpu.with_memory_space_constraint(back, pltpu.VMEM)
    done = {}
    for a in range(keep):
        kinds = [spaces.get((d, a), pltpu.HBM) for d in range(aux)]
        mine = apply(me[None], back, [fs[d, a] for d in range(aux)], kinds, a, width, per)
        for d in range(1, aux):
            done[d, a] = pltpu.with_memory_space_constraint(turn(mine, d), pltpu.VMEM)
        done[0, a] = mine
    done = [done[d, a] for a in range(keep) for d in range(aux)]
    return place(me[None], done, aux).T


def solution(mesh):
    return jax.shard_map(
        shards,
        mesh=mesh,
        in_specs=(P("basis", "aux", None), P("basis", None), P(), P(), P()),
        out_specs=P("basis", None),
        check_vma=False,
    )
```

```python
import functools

import jax
import jax.numpy as jnp
from jax import lax
from jax.experimental import pallas as pl
from jax.experimental.pallas import tpu as pltpu
from jax.sharding import PartitionSpec as P

BLOCK = 256
PAIR_CAP = 64
LANES = 128
VMEM = 56 * 1024 * 1024
NT = (((1,), (1,)), ((), ()))
F32 = jnp.float32
BF16 = jnp.bfloat16


def count_kernel(keep, slot_ref, pairs_ref, owner_ref, low_ref, high_ref, flag_ref):
    nblk = slot_ref.shape[1]
    npair = pairs_ref.shape[1]
    ids = lax.broadcasted_iota(jnp.int32, (nblk, npair), 0)
    owner = owner_ref[...]
    held = jnp.sum((owner == owner_ref[0:1, 0:1]).astype(F32), axis=1, keepdims=True)
    entry = lax.broadcasted_iota(jnp.int32, (1, npair), 1)
    weight = jnp.where(entry == 0, PAIR_CAP + 1.0 - held, 1.0)
    weight = jnp.where(owner >= 0, weight, 0.0)
    one_a = jnp.where(ids == pairs_ref[0:1, :], weight, 0.0).astype(BF16)
    one_b = (ids == pairs_ref[1:2, :]).astype(F32).astype(BF16)
    rows = lax.broadcasted_iota(jnp.int32, (nblk, nblk), 0)
    ndev = nblk // keep
    turned = (rows % ndev) * keep + rows // ndev

    def put(ids, one):
        place = (ids == slot_ref[...]).astype(F32).astype(BF16)
        return jnp.dot(place, one, preferred_element_type=F32).astype(BF16)

    count = lax.dot_general(put(turned, one_a), put(rows, one_b), NT, preferred_element_type=F32)
    count += lax.dot_general(put(turned, one_b), put(rows, one_a), NT, preferred_element_type=F32)
    high = jnp.floor(count * (1.0 / 256.0)) * 256.0
    low_ref[...] = (count - high).astype(BF16)
    high_ref[...] = high.astype(BF16)
    flag_ref[0] = (jnp.max(high) > 0).astype(jnp.int32)


def pair_counts(block_slot, pair_list, pair_owner, keep):
    nblk = block_slot.shape[0]
    square = jax.ShapeDtypeStruct((nblk, nblk), BF16)
    vmem = pl.BlockSpec(memory_space=pltpu.VMEM)
    return pl.pallas_call(
        functools.partial(count_kernel, keep),
        out_shape=(square, square, jax.ShapeDtypeStruct((1,), jnp.int32)),
        in_specs=[vmem] * 3,
        out_specs=(vmem, vmem, pl.BlockSpec(memory_space=pltpu.SMEM)),
        compiler_params=pltpu.CompilerParams(vmem_limit_bytes=VMEM),
        name="pair_counts",
    )(block_slot[None, :], pair_list.T, pair_owner[None, :])


def pack_kernel(per, me_ref, x_hbm, f_hbm, out_hbm, *refs):
    f_out, (x_ref, f_ref, out_ref, sems, out_sems, f_sems) = refs[:-6], refs[-6:]
    aux, span, width = x_ref.shape
    depth = f_ref.shape[1]
    keep = width // BLOCK
    full = depth // LANES
    rest = depth - full * LANES
    fold = LANES // rest
    group = -(-span // (fold * 8)) * 8
    step = span // per
    tail = out_ref.shape[0] - full * step

    def at(d, size):
        return pl.ds(pl.multiple_of(lax.rem(me_ref[0] + d, aux) * size, size), size)

    def fetch(d):
        return [
            pltpu.make_async_copy(src.at[:, at(d, width)], dst.at[d], sems.at[k, d])
            for k, (src, dst) in enumerate(((x_hbm, x_ref), (f_hbm, f_ref)))
        ]

    def send(d):
        rows = at(d, keep * per)
        return pltpu.make_async_copy(out_ref.at[:, rows], out_hbm.at[:, rows], out_sems.at[d])

    def pass_on(d):
        copies = []
        for a in range(keep):
            k = d * keep + a
            cols = slice(a * BLOCK, (a + 1) * BLOCK)
            copies.append(pltpu.make_async_copy(f_ref.at[d, :, cols], f_out[k], f_sems.at[k]))
        return copies

    order = list(range(1, aux)) + [0]
    for d in order:
        for copy in fetch(d):
            copy.start()
    for d in order:
        for copy in fetch(d):
            copy.wait()
        for copy in pass_on(d):
            copy.start()

        def product(k, lo, hi):
            cols = slice(k * BLOCK, (k + 1) * BLOCK)
            return lax.dot_general(
                x_ref[d, :, cols], f_ref[d, lo:hi, cols], NT, preferred_element_type=F32
            )

        place = at(d, keep * per)
        for t in range(0, full, 2):
            gs = [product(k, t * LANES, (t + 2) * LANES) for k in range(keep)]
            for half in range(2):
                lanes = slice(half * LANES, (half + 1) * LANES)
                rows = [g[:, lanes].reshape(step, per, LANES) for g in gs]
                first = (t + half) * step
                out_ref[first : first + step, place] = jnp.concatenate(rows, axis=1).astype(BF16)
        rows = []
        for k in range(keep):
            g = product(k, full * LANES, depth)
            g = jnp.concatenate([g, jnp.zeros((fold * group - span, rest), F32)], axis=0)
            g = jnp.concatenate([g[q * group : (q + 1) * group] for q in range(fold)], axis=1)
            g = jnp.concatenate([g, jnp.zeros((tail * per - group, LANES), F32)], axis=0)
            rows.append(g.reshape(tail, per, LANES))
        out_ref[full * step :, place] = jnp.concatenate(rows, axis=1).astype(BF16)
        send(d).start()
    for d in order:
        for copy in (*pass_on(d), send(d)):
            copy.wait()


def pack(me, xt, ft, ndev, aux, per):
    depth, rows = ft.shape
    blocks = rows // BLOCK
    width = rows // aux
    count = aux * (width // BLOCK)
    hbm = pl.BlockSpec(memory_space=pltpu.HBM)
    shape = jax.ShapeDtypeStruct((ndev, blocks * per, LANES), BF16)
    piece = jax.ShapeDtypeStruct((depth, BLOCK), BF16)
    return pl.pallas_call(
        functools.partial(pack_kernel, per),
        out_shape=[shape] + [piece] * count,
        in_specs=[pl.BlockSpec(memory_space=pltpu.SMEM), hbm, hbm],
        out_specs=[hbm] * (1 + count),
        scratch_shapes=[
            pltpu.VMEM((aux, xt.shape[0], width), BF16),
            pltpu.VMEM((aux, depth, width), BF16),
            pltpu.VMEM(shape.shape, BF16),
            pltpu.SemaphoreType.DMA((2, aux)),
            pltpu.SemaphoreType.DMA((aux,)),
            pltpu.SemaphoreType.DMA((count,)),
        ],
        compiler_params=pltpu.CompilerParams(vmem_limit_bytes=VMEM),
        name="pack",
    )(me, xt, ft)


def mix_kernel(
    per, flag_ref, low_hbm, high_hbm, g_ref, h_hbm, low_ref, high_ref, stage, turned, h_ref, sems, out_sems
):
    ndev, height, lanes = g_ref.shape
    blocks = height // per
    nblk = low_ref.shape[0]
    pitch = per + 1
    far = blocks * per + 1
    matrices = [
        pltpu.make_async_copy(low_hbm, low_ref, sems.at[0]),
        pltpu.make_async_copy(high_hbm, high_ref, sems.at[1]),
    ]
    for copy in matrices:
        copy.start()
    for c in range(ndev):
        v = g_ref[c].astype(F32)
        for b in range(blocks):
            stage[pl.ds((c * blocks + b) * pitch, per), :] = v[b * per : (b + 1) * per]
    for copy in matrices:
        copy.wait()

    def tiles(use_high):
        for t in range(0, per, 2):
            g = [stage[pl.ds(t + k, nblk, stride=pitch), :].astype(BF16) for k in range(2)]
            g = jnp.concatenate(g, axis=1)
            h = jnp.dot(low_ref[...], g, preferred_element_type=F32)
            if use_high:
                h += jnp.dot(high_ref[...], g, preferred_element_type=F32)
            for k in range(2):
                for a in range(blocks):
                    turned[pl.ds(a * per + t + k, ndev, stride=far), :] = h[
                        a * ndev : (a + 1) * ndev, k * lanes : (k + 1) * lanes
                    ]

    pl.when(flag_ref[0] == 0)(lambda: tiles(False))
    pl.when(flag_ref[0] != 0)(lambda: tiles(True))
    sends = out_sems.shape[0]
    group = ndev // sends

    def send(p):
        cut = slice(p * group, (p + 1) * group)
        return pltpu.make_async_copy(h_ref.at[cut], h_hbm.at[cut], out_sems.at[p])

    for p in range(sends):
        for i in range(p * group, (p + 1) * group):
            h_ref[i] = turned[i * far : i * far + height, :].astype(BF16)
        send(p).start()
    for p in range(sends):
        send(p).wait()


def mix(counts, g, per):
    low, high, flag = counts
    ndev, height, lanes = g.shape
    blocks = height // per
    vmem = pl.BlockSpec(memory_space=pltpu.VMEM)
    hbm = pl.BlockSpec(memory_space=pltpu.HBM)
    return pl.pallas_call(
        functools.partial(mix_kernel, per),
        out_shape=jax.ShapeDtypeStruct(g.shape, BF16),
        in_specs=[
            pl.BlockSpec(memory_space=pltpu.SMEM),
            hbm,
            hbm,
            vmem,
        ],
        out_specs=hbm,
        scratch_shapes=[
            pltpu.VMEM(low.shape, BF16),
            pltpu.VMEM(low.shape, BF16),
            pltpu.VMEM((ndev * blocks * (per + 1), lanes), F32),
            pltpu.VMEM((ndev * (height + 1), lanes), F32),
            pltpu.VMEM(g.shape, BF16),
            pltpu.SemaphoreType.DMA((2,)),
            pltpu.SemaphoreType.DMA((8,)),
        ],
        compiler_params=pltpu.CompilerParams(vmem_limit_bytes=VMEM),
        name="mix",
    )(flag, low, high, g)


def apply_kernel(per, a, me_ref, h_ref, *refs):
    f_refs, e_ref = refs[:-1], refs[-1]
    ndev, aux, height, lanes = h_ref.shape
    span = e_ref.shape[0]
    depth = f_refs[0].shape[0]
    full = depth // LANES
    rest = depth - full * LANES
    fold = LANES // rest
    group = -(-span // (fold * 8)) * 8
    step = span // per
    rows = slice(a * per, (a + 1) * per)
    total = jnp.zeros((span, BLOCK), F32)
    for d in range(aux):
        h = lax.rem(me_ref[0] + aux - d, aux)

        def take(lo, hi):
            v = h_ref[lo:hi, pl.ds(h, 1)].reshape(hi - lo, height, lanes).astype(F32)
            return v[:, rows].reshape(-1, lanes)

        left = [take(t * step, (t + 1) * step).astype(BF16) for t in range(full)]
        last = take(full * step, ndev)[:group]
        last = [last[:, q * rest : (q + 1) * rest] for q in range(fold)]
        last = jnp.concatenate(last, axis=0)[:span].astype(BF16)
        left = jnp.concatenate(left + [last], axis=1)
        total += jnp.dot(left, f_refs[d][...], preferred_element_type=F32)
    e_ref[...] = total.astype(BF16)


def apply(me, h, fs, a, span, per):
    vmem = pl.BlockSpec(memory_space=pltpu.VMEM)
    return pl.pallas_call(
        functools.partial(apply_kernel, per, a),
        out_shape=pltpu.VMEM((span, BLOCK), BF16),
        in_specs=[pl.BlockSpec(memory_space=pltpu.SMEM)] + [vmem] * (1 + len(fs)),
        out_specs=vmem,
        compiler_params=pltpu.CompilerParams(vmem_limit_bytes=VMEM),
        name="apply",
    )(me, h, *fs)


def place_kernel(aux, me_ref, *refs):
    pieces, out_hbm, sems = refs[:-2], refs[-2], refs[-1]
    keep = len(pieces) // aux
    copies = []
    for k, piece in enumerate(pieces):
        h = lax.rem(me_ref[0] + aux - k % aux, aux)
        start = pl.multiple_of((h * keep + k // aux) * BLOCK, BLOCK)
        copies.append(pltpu.make_async_copy(piece, out_hbm.at[:, pl.ds(start, BLOCK)], sems.at[k]))
    for copy in copies:
        copy.start()
    for copy in copies:
        copy.wait()


def place(me, pieces, aux):
    span, width = pieces[0].shape
    vmem = pl.BlockSpec(memory_space=pltpu.VMEM)
    return pl.pallas_call(
        functools.partial(place_kernel, aux),
        out_shape=jax.ShapeDtypeStruct((span, width * len(pieces)), BF16),
        in_specs=[pl.BlockSpec(memory_space=pltpu.SMEM)] + [vmem] * len(pieces),
        out_specs=pl.BlockSpec(memory_space=pltpu.HBM),
        scratch_shapes=[pltpu.SemaphoreType.DMA((len(pieces),))],
        compiler_params=pltpu.CompilerParams(vmem_limit_bytes=VMEM),
        name="place",
    )(me, *pieces)


def shards(factors, orbitals, block_slot, pair_list, pair_owner):
    ndev, aux = lax.axis_size("basis"), lax.axis_size("aux")
    me = lax.axis_index("aux").astype(jnp.int32)
    rows, aux_dev, width = factors.shape
    ft = factors.transpose(1, 2, 0).reshape(aux_dev * width, rows)
    xt = orbitals.T
    blocks = rows // BLOCK
    keep = blocks // aux
    per = -(-(aux_dev * width * width) // (LANES * ndev * 8)) * 8

    def turn(v, d):
        return lax.ppermute(v, "aux", [(k, (k + d) % aux) for k in range(aux)])

    sent, *pieces = pack(me[None], xt, ft, ndev, aux, per)
    got = lax.all_to_all(sent, "basis", split_axis=0, concat_axis=0, tiled=True)
    counts = pair_counts(block_slot, pair_list, pair_owner, blocks)
    far = aux // 2
    fs = {(d, a): turn(pieces[d * keep + a], d) for d in range(1, aux) for a in range(keep)}
    early = {k: v for k, v in fs.items() if k != (far, 0)}
    got, early = lax.optimization_barrier((got, early))
    fs.update(early)
    spaces = {k: pltpu.HBM if k in early else pltpu.VMEM for k in fs}
    fs = {k: pltpu.with_memory_space_constraint(v, spaces[k]) for k, v in fs.items()}
    fs.update({(0, a): pieces[a] for a in range(keep)})
    got = pltpu.with_memory_space_constraint(got, pltpu.VMEM)
    mixed = mix(counts, got, per)
    mixed = mixed.reshape(ndev * aux, -1, LANES)
    back = lax.all_to_all(mixed, ("basis", "aux"), split_axis=0, concat_axis=0, tiled=True)
    back = back.reshape(ndev, aux, *back.shape[1:])
    back = pltpu.with_memory_space_constraint(back, pltpu.VMEM)
    done = {}
    for a in range(keep):
        mine = apply(me[None], back, [fs[d, a] for d in range(aux)], a, width, per)
        for d in range(1, aux):
            done[d, a] = pltpu.with_memory_space_constraint(turn(mine, d), pltpu.VMEM)
        done[0, a] = mine
    done = [done[d, a] for a in range(keep) for d in range(aux)]
    return place(me[None], done, aux).T


def solution(mesh):
    return jax.shard_map(
        shards,
        mesh=mesh,
        in_specs=(P("basis", "aux", None), P("basis", None), P(), P(), P()),
        out_specs=P("basis", None),
        check_vma=False,
    )
```

```python
import functools

import jax
import jax.numpy as jnp
from jax import lax
from jax.experimental import pallas as pl
from jax.experimental.pallas import tpu as pltpu
from jax.sharding import PartitionSpec as P

BLOCK = 256
PAIR_CAP = 64
LANES = 128
VMEM = 56 * 1024 * 1024
NT = (((1,), (1,)), ((), ()))
F32 = jnp.float32
BF16 = jnp.bfloat16


def count_kernel(keep, slot_ref, pairs_ref, owner_ref, low_ref, high_ref, flag_ref):
    nblk = slot_ref.shape[1]
    npair = pairs_ref.shape[1]
    ids = lax.broadcasted_iota(jnp.int32, (nblk, npair), 0)
    owner = owner_ref[...]
    held = jnp.sum((owner == owner_ref[0:1, 0:1]).astype(F32), axis=1, keepdims=True)
    entry = lax.broadcasted_iota(jnp.int32, (1, npair), 1)
    weight = jnp.where(entry == 0, PAIR_CAP + 1.0 - held, 1.0)
    weight = jnp.where(owner >= 0, weight, 0.0)
    one_a = jnp.where(ids == pairs_ref[0:1, :], weight, 0.0).astype(BF16)
    one_b = (ids == pairs_ref[1:2, :]).astype(F32).astype(BF16)
    rows = lax.broadcasted_iota(jnp.int32, (nblk, nblk), 0)
    ndev = nblk // keep
    turned = (rows % ndev) * keep + rows // ndev

    def put(ids, one):
        place = (ids == slot_ref[...]).astype(F32).astype(BF16)
        return jnp.dot(place, one, preferred_element_type=F32).astype(BF16)

    count = lax.dot_general(put(turned, one_a), put(rows, one_b), NT, preferred_element_type=F32)
    count += lax.dot_general(put(turned, one_b), put(rows, one_a), NT, preferred_element_type=F32)
    high = jnp.floor(count * (1.0 / 256.0)) * 256.0
    low_ref[...] = (count - high).astype(BF16)
    high_ref[...] = high.astype(BF16)
    flag_ref[0] = (jnp.max(high) > 0).astype(jnp.int32)


def pair_counts(block_slot, pair_list, pair_owner, keep):
    nblk = block_slot.shape[0]
    square = jax.ShapeDtypeStruct((nblk, nblk), BF16)
    vmem = pl.BlockSpec(memory_space=pltpu.VMEM)
    return pl.pallas_call(
        functools.partial(count_kernel, keep),
        out_shape=(square, square, jax.ShapeDtypeStruct((1,), jnp.int32)),
        in_specs=[vmem] * 3,
        out_specs=(vmem, vmem, pl.BlockSpec(memory_space=pltpu.SMEM)),
        compiler_params=pltpu.CompilerParams(vmem_limit_bytes=VMEM),
        name="pair_counts",
    )(block_slot[None, :], pair_list.T, pair_owner[None, :])


def pack_kernel(per, me_ref, x_hbm, f_hbm, out_hbm, *refs):
    f_out, (x_ref, f_ref, out_ref, sems, out_sems, f_sems) = refs[:-6], refs[-6:]
    aux, span, width = x_ref.shape
    depth = f_ref.shape[1]
    keep = width // BLOCK
    full = depth // LANES
    rest = depth - full * LANES
    fold = LANES // rest
    group = -(-span // (fold * 8)) * 8
    step = span // per
    tail = out_ref.shape[0] - full * step

    def at(d, size):
        return pl.ds(pl.multiple_of(lax.rem(me_ref[0] + d, aux) * size, size), size)

    def fetch(d):
        return [
            pltpu.make_async_copy(src.at[:, at(d, width)], dst.at[d], sems.at[k, d])
            for k, (src, dst) in enumerate(((x_hbm, x_ref), (f_hbm, f_ref)))
        ]

    def send(d):
        rows = at(d, keep * per)
        return pltpu.make_async_copy(out_ref.at[:, rows], out_hbm.at[:, rows], out_sems.at[d])

    def pass_on(d):
        copies = []
        for a in range(keep):
            k = d * keep + a
            cols = slice(a * BLOCK, (a + 1) * BLOCK)
            copies.append(pltpu.make_async_copy(f_ref.at[d, :, cols], f_out[k], f_sems.at[k]))
        return copies

    order = list(range(1, aux)) + [0]
    for d in order:
        for copy in fetch(d):
            copy.start()
    for d in order:
        for copy in fetch(d):
            copy.wait()
        for copy in pass_on(d):
            copy.start()

        def product(k, lo, hi):
            cols = slice(k * BLOCK, (k + 1) * BLOCK)
            return lax.dot_general(
                x_ref[d, :, cols], f_ref[d, lo:hi, cols], NT, preferred_element_type=F32
            )

        place = at(d, keep * per)
        for t in range(0, full, 2):
            gs = [product(k, t * LANES, (t + 2) * LANES) for k in range(keep)]
            for half in range(2):
                lanes = slice(half * LANES, (half + 1) * LANES)
                rows = [g[:, lanes].reshape(step, per, LANES) for g in gs]
                first = (t + half) * step
                out_ref[first : first + step, place] = jnp.concatenate(rows, axis=1).astype(BF16)
        rows = []
        for k in range(keep):
            g = product(k, full * LANES, depth)
            g = jnp.concatenate([g, jnp.zeros((fold * group - span, rest), F32)], axis=0)
            g = jnp.concatenate([g[q * group : (q + 1) * group] for q in range(fold)], axis=1)
            g = jnp.concatenate([g, jnp.zeros((tail * per - group, LANES), F32)], axis=0)
            rows.append(g.reshape(tail, per, LANES))
        out_ref[full * step :, place] = jnp.concatenate(rows, axis=1).astype(BF16)
        send(d).start()
    for d in order:
        for copy in (*pass_on(d), send(d)):
            copy.wait()


def pack(me, xt, ft, ndev, aux, per):
    depth, rows = ft.shape
    blocks = rows // BLOCK
    width = rows // aux
    count = aux * (width // BLOCK)
    hbm = pl.BlockSpec(memory_space=pltpu.HBM)
    shape = jax.ShapeDtypeStruct((ndev, blocks * per, LANES), BF16)
    piece = jax.ShapeDtypeStruct((depth, BLOCK), BF16)
    return pl.pallas_call(
        functools.partial(pack_kernel, per),
        out_shape=[shape] + [piece] * count,
        in_specs=[pl.BlockSpec(memory_space=pltpu.SMEM), hbm, hbm],
        out_specs=[hbm] * (1 + count),
        scratch_shapes=[
            pltpu.VMEM((aux, xt.shape[0], width), BF16),
            pltpu.VMEM((aux, depth, width), BF16),
            pltpu.VMEM(shape.shape, BF16),
            pltpu.SemaphoreType.DMA((2, aux)),
            pltpu.SemaphoreType.DMA((aux,)),
            pltpu.SemaphoreType.DMA((count,)),
        ],
        compiler_params=pltpu.CompilerParams(vmem_limit_bytes=VMEM),
        name="pack",
    )(me, xt, ft)


def mix_kernel(
    per, flag_ref, low_hbm, high_hbm, g_ref, h_hbm, low_ref, high_ref, stage, turned, h_ref, sems, out_sems
):
    ndev, height, lanes = g_ref.shape
    blocks = height // per
    nblk = low_ref.shape[0]
    pitch = per + 1
    far = blocks * per + 1
    matrices = [
        pltpu.make_async_copy(low_hbm, low_ref, sems.at[0]),
        pltpu.make_async_copy(high_hbm, high_ref, sems.at[1]),
    ]
    for copy in matrices:
        copy.start()
    for c in range(ndev):
        v = g_ref[c].astype(F32)
        for b in range(blocks):
            stage[pl.ds((c * blocks + b) * pitch, per), :] = v[b * per : (b + 1) * per]
    for copy in matrices:
        copy.wait()

    def tiles(use_high):
        for t in range(0, per, 2):
            g = [stage[pl.ds(t + k, nblk, stride=pitch), :].astype(BF16) for k in range(2)]
            g = jnp.concatenate(g, axis=1)
            h = jnp.dot(low_ref[...], g, preferred_element_type=F32)
            if use_high:
                h += jnp.dot(high_ref[...], g, preferred_element_type=F32)
            for k in range(2):
                for a in range(blocks):
                    turned[pl.ds(a * per + t + k, ndev, stride=far), :] = h[
                        a * ndev : (a + 1) * ndev, k * lanes : (k + 1) * lanes
                    ]

    pl.when(flag_ref[0] == 0)(lambda: tiles(False))
    pl.when(flag_ref[0] != 0)(lambda: tiles(True))
    sends = out_sems.shape[0]
    group = ndev // sends

    def send(p):
        cut = slice(p * group, (p + 1) * group)
        return pltpu.make_async_copy(h_ref.at[cut], h_hbm.at[cut], out_sems.at[p])

    for p in range(sends):
        for i in range(p * group, (p + 1) * group):
            h_ref[i] = turned[i * far : i * far + height, :].astype(BF16)
        send(p).start()
    for p in range(sends):
        send(p).wait()


def mix(counts, g, per):
    low, high, flag = counts
    ndev, height, lanes = g.shape
    blocks = height // per
    vmem = pl.BlockSpec(memory_space=pltpu.VMEM)
    hbm = pl.BlockSpec(memory_space=pltpu.HBM)
    return pl.pallas_call(
        functools.partial(mix_kernel, per),
        out_shape=jax.ShapeDtypeStruct(g.shape, BF16),
        in_specs=[
            pl.BlockSpec(memory_space=pltpu.SMEM),
            hbm,
            hbm,
            vmem,
        ],
        out_specs=hbm,
        scratch_shapes=[
            pltpu.VMEM(low.shape, BF16),
            pltpu.VMEM(low.shape, BF16),
            pltpu.VMEM((ndev * blocks * (per + 1), lanes), F32),
            pltpu.VMEM((ndev * (height + 1), lanes), F32),
            pltpu.VMEM(g.shape, BF16),
            pltpu.SemaphoreType.DMA((2,)),
            pltpu.SemaphoreType.DMA((4,)),
        ],
        compiler_params=pltpu.CompilerParams(vmem_limit_bytes=VMEM),
        name="mix",
    )(flag, low, high, g)


def apply_kernel(per, a, me_ref, h_ref, *refs):
    f_refs, e_ref = refs[:-1], refs[-1]
    ndev, aux, height, lanes = h_ref.shape
    span = e_ref.shape[0]
    depth = f_refs[0].shape[0]
    full = depth // LANES
    rest = depth - full * LANES
    fold = LANES // rest
    group = -(-span // (fold * 8)) * 8
    step = span // per
    rows = slice(a * per, (a + 1) * per)
    total = jnp.zeros((span, BLOCK), F32)
    for d in range(aux):
        h = lax.rem(me_ref[0] + aux - d, aux)

        def take(lo, hi):
            v = h_ref[lo:hi, pl.ds(h, 1)].reshape(hi - lo, height, lanes).astype(F32)
            return v[:, rows].reshape(-1, lanes)

        left = [take(t * step, (t + 1) * step).astype(BF16) for t in range(full)]
        last = take(full * step, ndev)[:group]
        last = [last[:, q * rest : (q + 1) * rest] for q in range(fold)]
        last = jnp.concatenate(last, axis=0)[:span].astype(BF16)
        left = jnp.concatenate(left + [last], axis=1)
        total += jnp.dot(left, f_refs[d][...], preferred_element_type=F32)
    e_ref[...] = total.astype(BF16)


def apply(me, h, fs, a, span, per):
    vmem = pl.BlockSpec(memory_space=pltpu.VMEM)
    return pl.pallas_call(
        functools.partial(apply_kernel, per, a),
        out_shape=pltpu.VMEM((span, BLOCK), BF16),
        in_specs=[pl.BlockSpec(memory_space=pltpu.SMEM)] + [vmem] * (1 + len(fs)),
        out_specs=vmem,
        compiler_params=pltpu.CompilerParams(vmem_limit_bytes=VMEM),
        name="apply",
    )(me, h, *fs)


def place_kernel(aux, me_ref, *refs):
    pieces, out_hbm, sems = refs[:-2], refs[-2], refs[-1]
    keep = len(pieces) // aux
    copies = []
    for k, piece in enumerate(pieces):
        h = lax.rem(me_ref[0] + aux - k % aux, aux)
        start = pl.multiple_of((h * keep + k // aux) * BLOCK, BLOCK)
        copies.append(pltpu.make_async_copy(piece, out_hbm.at[:, pl.ds(start, BLOCK)], sems.at[k]))
    for copy in copies:
        copy.start()
    for copy in copies:
        copy.wait()


def place(me, pieces, aux):
    span, width = pieces[0].shape
    vmem = pl.BlockSpec(memory_space=pltpu.VMEM)
    return pl.pallas_call(
        functools.partial(place_kernel, aux),
        out_shape=jax.ShapeDtypeStruct((span, width * len(pieces)), BF16),
        in_specs=[pl.BlockSpec(memory_space=pltpu.SMEM)] + [vmem] * len(pieces),
        out_specs=pl.BlockSpec(memory_space=pltpu.HBM),
        scratch_shapes=[pltpu.SemaphoreType.DMA((len(pieces),))],
        compiler_params=pltpu.CompilerParams(vmem_limit_bytes=VMEM),
        name="place",
    )(me, *pieces)


def shards(factors, orbitals, block_slot, pair_list, pair_owner):
    ndev, aux = lax.axis_size("basis"), lax.axis_size("aux")
    me = lax.axis_index("aux").astype(jnp.int32)
    rows, aux_dev, width = factors.shape
    ft = factors.transpose(1, 2, 0).reshape(aux_dev * width, rows)
    xt = orbitals.T
    blocks = rows // BLOCK
    keep = blocks // aux
    per = -(-(aux_dev * width * width) // (LANES * ndev * 8)) * 8

    def turn(v, d):
        return lax.ppermute(v, "aux", [(k, (k + d) % aux) for k in range(aux)])

    sent, *pieces = pack(me[None], xt, ft, ndev, aux, per)
    got = lax.all_to_all(sent, "basis", split_axis=0, concat_axis=0, tiled=True)
    counts = pair_counts(block_slot, pair_list, pair_owner, blocks)
    far = aux // 2
    fs = {(d, a): turn(pieces[d * keep + a], d) for d in range(1, aux) for a in range(keep)}
    early = {k: v for k, v in fs.items() if k != (far, 0)}
    got, early = lax.optimization_barrier((got, early))
    fs.update(early)
    spaces = {k: pltpu.HBM if k in early else pltpu.VMEM for k in fs}
    fs = {k: pltpu.with_memory_space_constraint(v, spaces[k]) for k, v in fs.items()}
    fs.update({(0, a): pieces[a] for a in range(keep)})
    got = pltpu.with_memory_space_constraint(got, pltpu.VMEM)
    mixed = mix(counts, got, per)
    mixed = mixed.reshape(ndev * aux, -1, LANES)
    back = lax.all_to_all(mixed, ("basis", "aux"), split_axis=0, concat_axis=0, tiled=True)
    back = back.reshape(ndev, aux, *back.shape[1:])
    back = pltpu.with_memory_space_constraint(back, pltpu.VMEM)
    done = {}
    for a in range(keep):
        mine = apply(me[None], back, [fs[d, a] for d in range(aux)], a, width, per)
        for d in range(1, aux):
            done[d, a] = pltpu.with_memory_space_constraint(turn(mine, d), pltpu.VMEM)
        done[0, a] = mine
    done = [done[d, a] for a in range(keep) for d in range(aux)]
    return place(me[None], done, aux).T


def solution(mesh):
    return jax.shard_map(
        shards,
        mesh=mesh,
        in_specs=(P("basis", "aux", None), P("basis", None), P(), P(), P()),
        out_specs=P("basis", None),
        check_vma=False,
    )
```
